512 devices in a mesh: date: 256 (over z, y, x), row: 2 (over core).
Axes of the slice: x: 4, y: 8, z: 8, core: 2. Of those that a mesh axis runs over, the one named last changes fastest.
Arguments:
- slc: bfloat16 [2, 256, 32, 1024], P(None, 'date', 'row'), may hold values from -6 to 6
- valid_rows: int32 [256, 32], P('date', 'row'), may hold values 0 or 1
- pair_order: int32 [256, 10], P('date'), may hold values from 0 to 9, each once within a row
Outputs:
- phase: bfloat16 [2, 256, 10, 32, 1024], P(None, 'date', None, 'row')
- coherence: bfloat16 [256, 10, 32, 1024], P('date', None, 'row')
The draws below stay inside these ranges and needn't reach their ends.
Inputs may be any that keep to these rules, and one draw needn't show every extreme that they name: `pair_order`: each date's row holds every value from 0 to 9 once.
All inputs are finite; a program needn't handle non-finite values. No bound on the sum of `valid_rows` on one device may be relied on, other than what follows from the above.
Results may differ from the reference program's by a relative error of at most 0.001.
Values may be sent and summed in bfloat16 or wider, within the bound.
No kernel may reach another device: no remote copies, remote signals or barrier semaphores. Data moves between devices by JAX's collectives and lax.ppermute only.
A program may use at most 64 MiB of HBM per device.

```python
import jax
import jax.numpy as jnp
from jax import lax

COLS = 1024
BAND = 10
DATES = 256
ROWS = 32


def with_ends(values, key, smallest, largest):
    longest = values.shape.index(max(values.shape))
    spots = []
    for shift in (0, 1):
        where = [jax.random.randint(jax.random.fold_in(key, axis), (), 0, length) for axis, length in enumerate(values.shape)]
        where[longest] = (where[longest] + shift) % values.shape[longest]
        spots.append(tuple(where))
    return values.at[spots[0]].set(smallest).at[spots[1]].set(largest)


def steps_of(rng, dims, split, smallest, top_value):
    def one(position, shards_of):
        heights = jax.random.uniform(jax.random.fold_in(jax.random.fold_in(rng, 6), position), (shards_of,), jnp.float32, smallest / len(split), top_value / len(split))
        return jnp.repeat(jnp.exp(heights), dims[position] // shards_of).reshape((-1,) + (1,) * (len(dims) - position - 1))

    factor_of = one(*split[0])
    for cut in split[1:]:
        factor_of = factor_of * one(*cut)
    return factor_of


def gaussian(own_key, shape, width, reach, split=(), kind=jnp.bfloat16):
    drawn = width * jax.random.normal(own_key, shape, jnp.float32)
    if split:
        drawn = drawn * steps_of(own_key, shape, split, -0.22, 0.18)
    return jnp.clip(drawn, -reach, reach).astype(kind)


def setup_inputs(seed: int = 0) -> dict:
    splits = jax.random.split(jax.random.key(seed), 4)
    return {
        "slc": gaussian(splits[0], (2, DATES, ROWS, COLS), 1.0, 6.0, ((1, 256), (2, 2))),
        "valid_rows": with_ends((jax.random.randint(splits[1], (DATES, ROWS), 0, 16) < 15).astype(jnp.int32), jax.random.fold_in(splits[1], 1), 0, 1),
        "pair_order": jax.vmap(lambda own: jax.random.permutation(own, BAND))(jax.random.split(splits[2], DATES)).reshape((DATES, BAND)).astype(jnp.int32),
    }


def window_sum(values):
    padded = jnp.pad(values, ((0, 0), (3, 3), (3, 3)))
    zero = jnp.array(0, values.dtype)
    return lax.reduce_window(padded, zero, lax.add, (1, 7, 7), (1, 1, 1), 'VALID')

def reference(slc, valid_rows, pair_order):
    slab = slc * valid_rows.astype(jnp.bfloat16)[None, :, :, None]
    extra = jnp.zeros((2, BAND, ROWS, COLS), jnp.bfloat16)
    full = jnp.concatenate([slab, extra], axis=1)
    wide = full.astype(jnp.float32)
    inten_sums = window_sum(wide[0] * wide[0] + wide[1] * wide[1])

    def one_date(date):
        partners = date + 1 + pair_order[date]
        other = jnp.take(full, partners, axis=1).astype(jnp.float32)
        own = lax.dynamic_index_in_dim(full, date, 1, keepdims=False).astype(jnp.float32)
        prod_re = own[0][None] * other[0] + own[1][None] * other[1]
        prod_im = own[1][None] * other[0] - own[0][None] * other[1]
        sum_re = window_sum(prod_re)
        sum_im = window_sum(prod_im)
        first_sum = lax.dynamic_index_in_dim(inten_sums, date, 0, keepdims=False)
        second_sum = jnp.take(inten_sums, partners, axis=0)
        magnitude = jnp.sqrt(sum_re * sum_re + sum_im * sum_im)
        scale = 1.0 / jnp.maximum(magnitude, 1.0)
        cosine = (sum_re * scale).astype(jnp.bfloat16)
        sine = (sum_im * scale).astype(jnp.bfloat16)
        coher = magnitude / jnp.sqrt(jnp.maximum(first_sum[None] * second_sum, 1.0))
        return (cosine, sine, coher.astype(jnp.bfloat16))
    cosine, sine, coher = lax.map(one_date, jnp.arange(DATES, dtype=jnp.int32))
    return (jnp.stack([cosine, sine]), coher)
```

```python
import jax
import jax.numpy as jnp
from jax import lax
from jax.experimental import pallas as pl
from jax.experimental.pallas import tpu as pltpu
from jax.sharding import PartitionSpec as P

GROUP = 8
HALO = 3
BLOCK = 128


def shifted(shard, by):
    length = lax.axis_size("date")
    return lax.ppermute(shard, "date", [(i, i - by) for i in range(by, length)])


def vertical(rows):
    count = rows.shape[0] - 6
    two = rows[:-1] + rows[1:]
    four = two[:-2] + two[2:]
    return four[:count] + two[4 : 4 + count] + rows[6 : 6 + count]


def moved(x, by, before, after):
    lane = lax.broadcasted_iota(jnp.int32, x.shape, 2)
    if by > 0:
        near = jnp.concatenate([before, x[:-1]], axis=0)
        mixed = jnp.where(lane >= BLOCK - by, near, x)
    else:
        near = jnp.concatenate([x[1:], after], axis=0)
        mixed = jnp.where(lane < -by, near, x)
    return pltpu.roll(mixed, by % BLOCK, 2)


def horizontal(x):
    zero = jnp.zeros_like(x[:1])
    lane = lax.broadcasted_iota(jnp.int32, zero.shape, 2)
    three = x + moved(x, 1, zero, zero) + moved(x, -1, zero, zero)
    before = jnp.where(lane == BLOCK - 1, pltpu.roll(x[:1], BLOCK - 1, 2), zero)
    after = jnp.where(lane == 0, pltpu.roll(x[-1:], 1, 2), zero)
    return x + moved(three, 2, before, after) + moved(three, -2, before, after)


def kernel(order, place, own, near, nine, ten, phase, coher, slots, padded, sums, first):
    own_rows, cells = own.shape[0], 8
    height = own_rows - HALO
    blocks = phase.shape[-1] // BLOCK
    core, rank = place[0], place[1]
    start = HALO * (1 - core)
    band = order.shape[1]
    for j in range(band):
        slots[order[0, j]] = j
    padded[...] = jnp.zeros_like(padded)

    def box_to(index, values):
        padded[index, pl.ds(start, own_rows)] = values

    def columns(index):
        chunk = 4
        for base in range(0, height, chunk):
            got = vertical(padded[index, base : base + chunk + 6])
            for i in range(chunk):
                sums[index, pl.ds(base + i, blocks, stride=height), :] = got[i]

    def summed(index, half):
        x = sums[index].reshape(blocks, height, BLOCK)[:, half * 8 : half * 8 + 8]
        return horizontal(x)

    def intensity(pair):
        return pair[:, :cells] * pair[:, :cells] + pair[:, cells:] * pair[:, cells:]

    mine = own[...].astype(jnp.float32)
    box_to(2, intensity(mine))
    columns(2)
    for half in range(height // 8):
        first[:, half * 8 : half * 8 + 8] = summed(2, half)

    def one(other, offset):
        slot = slots[offset - 1]
        a = own[...].astype(jnp.float32)
        b = other.astype(jnp.float32)
        a0, a1, b0, b1 = a[:, :cells], a[:, cells:], b[:, :cells], b[:, cells:]
        box_to(0, a0 * b0 + a1 * b1)
        box_to(1, a1 * b0 - a0 * b1)
        box_to(2, b0 * b0 + b1 * b1)
        for index in range(3):
            columns(index)
        res = [[], [], []]
        for half in range(height // 8):
            re, im, second = (summed(index, half) for index in range(3))
            power = re * re + im * im
            scale = lax.rsqrt(jnp.maximum(power, 1.0))
            both = first[:, half * 8 : half * 8 + 8] * second
            co = jnp.sqrt(power) * lax.rsqrt(jnp.maximum(both, 1.0))
            for kept, value in zip(res, (re * scale, im * scale, co)):
                kept.append(value)
        re, im, co = (jnp.concatenate(kept, axis=1).astype(jnp.bfloat16) for kept in res)
        for b in range(blocks):
            at = slice(b * BLOCK, (b + 1) * BLOCK)
            phase[0, slot, :, at] = re[b]
            phase[1, slot, :, at] = im[b]
            coher[slot, :, at] = co[b]

    def step(p, carry):
        offset = lax.rem(p - rank + GROUP - 1, GROUP) + 1
        one(near[p], offset)
        return carry

    lax.fori_loop(0, GROUP, step, 0)
    one(nine[...], 9)
    one(ten[...], 10)


def shards(slc, valid_rows, pair_order):
    _, _, height, width = slc.shape
    band = pair_order.shape[1]
    blocks = width // BLOCK
    cells = 2 * blocks
    core = lax.axis_index("row")
    rank = lax.rem(lax.axis_index("date"), GROUP)
    slab = slc[:, 0] * valid_rows.astype(jnp.bfloat16)[0][None, :, None]
    slab = slab.reshape(2, height, blocks, BLOCK).transpose(1, 0, 2, 3).reshape(height, cells, BLOCK)
    edge = lax.dynamic_slice_in_dim(slab, (height - HALO) * (1 - core), HALO, axis=0)
    halo = lax.ppermute(edge, "row", [(0, 1), (1, 0)])
    own = jnp.where(
        core == 0,
        jnp.concatenate([slab, halo], axis=0),
        jnp.concatenate([halo, slab], axis=0),
    )
    eight = shifted(own, 8)
    nine = shifted(own, 9)
    ten = shifted(own, 10)
    members = jnp.arange(GROUP)[:, None, None, None]
    given = jnp.where(members < rank, own[None], eight[None])
    length = lax.axis_size("date")
    groups = [list(range(g, g + GROUP)) for g in range(0, length, GROUP)]
    near = lax.all_to_all(given, "date", 0, 0, axis_index_groups=groups, tiled=True)
    place = jnp.stack([core, rank]).astype(jnp.int32)
    rows = height + HALO
    whole = pl.BlockSpec(memory_space=pltpu.VMEM)
    scalars = pl.BlockSpec(memory_space=pltpu.SMEM)
    phase, coher = pl.pallas_call(
        kernel,
        out_shape=(
            jax.ShapeDtypeStruct((2, band, height, width), jnp.bfloat16),
            jax.ShapeDtypeStruct((band, height, width), jnp.bfloat16),
        ),
        in_specs=[scalars, scalars, whole, whole, whole, whole],
        out_specs=(whole, whole),
        scratch_shapes=[
            pltpu.SMEM((band,), jnp.int32),
            pltpu.VMEM((3, height + 2 * HALO, blocks, BLOCK), jnp.float32),
            pltpu.VMEM((3, blocks * height, BLOCK), jnp.float32),
            pltpu.VMEM((blocks, height, BLOCK), jnp.float32),
        ],
        compiler_params=pltpu.CompilerParams(vmem_limit_bytes=24 << 20),
        cost_estimate=pl.CostEstimate(flops=20 << 20, bytes_accessed=3 << 20, transcendentals=1 << 19),
    )(pair_order, place, own, near, nine, ten)
    return phase[:, None], coher[None]


def solution(mesh):
    placed = (P(None, "date", "row", None), P("date", "row"), P("date", None))
    return jax.shard_map(
        shards,
        mesh=mesh,
        in_specs=placed,
        out_specs=(P(None, "date", None, "row", None), P("date", None, "row", None)),
        check_vma=False,
    )
```

```python
import jax
import jax.numpy as jnp
from jax import lax
from jax.experimental import pallas as pl
from jax.experimental.pallas import tpu as pltpu
from jax.sharding import PartitionSpec as P

GROUP = 8
HALO = 3
BLOCK = 128
TINY = 1.1754944e-38
WHOLE = pl.BlockSpec(memory_space=pltpu.VMEM)
SCALARS = pl.BlockSpec(memory_space=pltpu.SMEM)
AWAY = pl.BlockSpec(memory_space=pl.ANY)


class Column:
    def __init__(self):
        self.rows, self.two, self.four = [], [], []

    def feed(self, row):
        rows, two, four = self.rows, self.two, self.four
        rows.append(row)
        at = len(rows) - 1
        if at >= 1:
            two.append(rows[at - 1] + row)
        if at >= 3:
            four.append(two[at - 3] + two[at - 1])
        out = at - HALO
        if out < 0:
            return None
        if out == 0:
            return four[0]
        if out == 1:
            return four[0] + rows[4]
        if out == 2:
            return four[0] + two[4]
        return four[out - 3] + two[out + 1] + row


def band_matrix(ref):
    shape = (BLOCK, 2 * BLOCK)
    source = lax.broadcasted_iota(jnp.int32, shape, 0)
    target = lax.broadcasted_iota(jnp.int32, shape, 1)
    gap = jnp.where(target < BLOCK, jnp.abs(target - source), BLOCK - jnp.abs(target - BLOCK - source))
    ones = (gap <= HALO).astype(jnp.float32).astype(jnp.bfloat16)
    for part in range(3):
        ref[part * BLOCK : (part + 1) * BLOCK, :] = ones


def horizontal(x, band):
    count, blocks, height, _ = x.shape
    x = x.reshape(count * blocks * height, BLOCK)
    high = x.astype(jnp.bfloat16)
    rest = x - high.astype(jnp.float32)
    middle = rest.astype(jnp.bfloat16)
    low = (rest - middle.astype(jnp.float32)).astype(jnp.bfloat16)
    parts = jnp.concatenate([high, middle, low], axis=1)
    got = jnp.dot(parts, band, preferred_element_type=jnp.float32)
    got = got.reshape(count, blocks, height, 2 * BLOCK)
    inside, beside = got[..., :BLOCK], got[..., BLOCK:]
    zero = jnp.zeros_like(beside[:, :1])
    before = jnp.concatenate([zero, beside[:, :-1]], axis=1)
    after = jnp.concatenate([beside[:, 1:], zero], axis=1)
    lane = lax.broadcasted_iota(jnp.int32, beside.shape, 3)
    return inside + jnp.where(lane < BLOCK // 2, before, after)


class Pairs:
    def __init__(self, order, place, own, phase, coher, slots, mine, band, staged, sems):
        self.core = place[0]
        self.phase, self.coher = phase, coher
        self.slots, self.mine, self.band, self.staged, self.sems = slots, mine, band, staged, sems
        self.rows, self.cells = own.shape[0], own.shape[1] // 2
        self.height, self.blocks = self.rows - HALO, own.shape[1] // 2
        for j in range(order.shape[1]):
            slots[order[0, j]] = j
        for row in range(self.rows):
            mine[row] = own[row].astype(jnp.float32)
        band_matrix(band)

    def store(self, sums, index, row, value):
        if value is not None:
            out = row - HALO
            spot = out + self.core * (self.height - 1 - 2 * out)
            sums[index, pl.ds(spot, self.blocks, stride=self.height), :] = value

    def boxes(self, sums, count):
        x = sums[:count].reshape(count, self.blocks, self.height, BLOCK)
        return horizontal(x, self.band[...])

    def own_intensity(self, sums, first):
        column = Column()
        for row in range(self.rows):
            a0, a1 = self.mine[row, : self.cells], self.mine[row, self.cells :]
            self.store(sums, 0, row, column.feed(a0 * a0 + a1 * a1))
        first[...] = self.boxes(sums, 1)[0]

    def copies(self, turn, slot):
        kept, sems = self.staged.at[turn], self.sems.at[turn]
        return (
            pltpu.make_async_copy(kept.at[0:2], self.phase.at[:, slot], sems.at[0]),
            pltpu.make_async_copy(kept.at[2], self.coher.at[slot], sems.at[1]),
        )

    def one(self, other, offset, turn, sums, first):
        slot = self.slots[offset - 1]
        columns = [Column() for _ in range(3)]
        for row in range(self.rows):
            a0, a1 = self.mine[row, : self.cells], self.mine[row, self.cells :]
            b = other[row].astype(jnp.float32)
            b0, b1 = b[: self.cells], b[self.cells :]
            values = (a0 * b0 + a1 * b1, a1 * b0 - a0 * b1, b0 * b0 + b1 * b1)
            for index, value in enumerate(values):
                self.store(sums, index, row, columns[index].feed(value))
        re, im, second = self.boxes(sums, 3)
        power = re * re + im * im
        inverse = lax.rsqrt(jnp.maximum(power, TINY))
        scale = jnp.minimum(inverse, 1.0)
        both = first[...] * second
        co = power * inverse * lax.rsqrt(jnp.maximum(both, 1.0))
        for index, value in enumerate((re * scale, im * scale, co)):
            value = value.astype(jnp.bfloat16)
            for b in range(self.blocks):
                self.staged[turn, index, :, b * BLOCK : (b + 1) * BLOCK] = value[b]
        for copy in self.copies(turn, slot):
            copy.start()

    def finish(self, turns):
        for turn in range(turns):
            for copy in self.copies(turn, 0):
                copy.wait()


def first_kernel(order, place, own, eight, phase, coher, first, slots, mine, band, staged, sems, *sums):
    pairs = Pairs(order, place, own, phase, coher, slots, mine, band, staged, sems)
    pairs.own_intensity(sums[1], first)
    pairs.one(eight, GROUP, 0, sums[0], first)
    pairs.finish(1)


def near_kernel(order, place, own, near, first, _p, _c, phase, coher, slots, mine, band, staged, sems, *sums):
    pairs = Pairs(order, place, own, phase, coher, slots, mine, band, staged, sems)
    for turn in range(GROUP - 1):
        member = lax.rem(place[1] + 1 + turn, GROUP)
        pairs.one(near.at[member], turn + 1, turn, sums[turn % len(sums)], first)
    pairs.finish(GROUP - 1)


def last_kernel(order, place, own, nine, ten, first, _p, _c, phase, coher, slots, mine, band, staged, sems, *sums):
    pairs = Pairs(order, place, own, phase, coher, slots, mine, band, staged, sems)
    pairs.one(nine, GROUP + 1, 0, sums[0], first)
    pairs.one(ten, GROUP + 2, 1, sums[1], first)
    pairs.finish(2)


def shifted(shard, by):
    length = lax.axis_size("date")
    return lax.ppermute(shard, "date", [(i, i - by) for i in range(by, length)])


def shards(slc, valid_rows, pair_order):
    _, _, height, width = slc.shape
    band = pair_order.shape[1]
    blocks = width // BLOCK
    cells = 2 * blocks
    rows = height + HALO
    core = lax.axis_index("row")
    rank = lax.rem(lax.axis_index("date"), GROUP)
    length = lax.axis_size("date")
    slab = slc[:, 0] * valid_rows.astype(jnp.bfloat16)[0][None, :, None]
    slab = slab.reshape(2, height, blocks, BLOCK).transpose(1, 0, 2, 3).reshape(height, cells, BLOCK)
    slab = jnp.where(core == 0, slab, slab[::-1])
    halo = lax.ppermute(slab[height - HALO :][::-1], "row", [(0, 1), (1, 0)])
    own = jnp.concatenate([slab, halo], axis=0)
    eight = shifted(own, GROUP)
    members = jnp.arange(GROUP)[:, None, None, None]
    given = jnp.where(members < rank, own[None], eight[None])
    groups = [list(range(g, g + GROUP)) for g in range(0, length, GROUP)]
    near = lax.all_to_all(given, "date", 0, 0, axis_index_groups=groups, tiled=True)
    nine = shifted(eight, 1)
    ten = shifted(eight, 2)
    place = jnp.stack([core, rank]).astype(jnp.int32)

    outs = (
        jax.ShapeDtypeStruct((2, band, height, width), jnp.bfloat16),
        jax.ShapeDtypeStruct((band, height, width), jnp.bfloat16),
    )
    kept = jax.ShapeDtypeStruct((blocks, height, BLOCK), jnp.float32)

    def scratch(turns, buffers):
        return [
            pltpu.SMEM((band,), jnp.int32),
            pltpu.VMEM((rows, cells, BLOCK), jnp.float32),
            pltpu.VMEM((3 * BLOCK, 2 * BLOCK), jnp.bfloat16),
            pltpu.VMEM((turns, 3, height, width), jnp.bfloat16),
            pltpu.SemaphoreType.DMA((turns, 2)),
        ] + [pltpu.VMEM((3, blocks * height, BLOCK), jnp.float32) for _ in range(buffers)]

    def cost(count):
        return pl.CostEstimate(flops=count << 23, bytes_accessed=count << 18, transcendentals=count << 15)

    params = pltpu.CompilerParams(vmem_limit_bytes=16 << 20)
    phase, coher, first = pl.pallas_call(
        first_kernel,
        out_shape=outs + (kept,),
        in_specs=[SCALARS, SCALARS, WHOLE, WHOLE],
        out_specs=(AWAY, AWAY, WHOLE),
        scratch_shapes=scratch(1, 2),
        compiler_params=params,
        cost_estimate=cost(1),
    )(pair_order, place, own, eight)
    phase, coher = pl.pallas_call(
        near_kernel,
        out_shape=outs,
        in_specs=[SCALARS, SCALARS, WHOLE, WHOLE, WHOLE, AWAY, AWAY],
        out_specs=(AWAY, AWAY),
        scratch_shapes=scratch(GROUP - 1, 2),
        input_output_aliases={5: 0, 6: 1},
        compiler_params=params,
        cost_estimate=cost(GROUP - 1),
    )(pair_order, place, own, near, first, phase, coher)
    phase, coher = pl.pallas_call(
        last_kernel,
        out_shape=outs,
        in_specs=[SCALARS, SCALARS, WHOLE, WHOLE, WHOLE, WHOLE, AWAY, AWAY],
        out_specs=(AWAY, AWAY),
        scratch_shapes=scratch(2, 2),
        input_output_aliases={6: 0, 7: 1},
        compiler_params=params,
        cost_estimate=cost(2),
    )(pair_order, place, own, nine, ten, first, phase, coher)
    return phase[:, None], coher[None]


def solution(mesh):
    placed = (P(None, "date", "row", None), P("date", "row"), P("date", None))
    return jax.shard_map(
        shards,
        mesh=mesh,
        in_specs=placed,
        out_specs=(P(None, "date", None, "row", None), P("date", None, "row", None)),
        check_vma=False,
    )
```

```python
import jax
import jax.numpy as jnp
from jax import lax
from jax.experimental import pallas as pl
from jax.experimental.pallas import tpu as pltpu
from jax.sharding import PartitionSpec as P

GROUP = 8
PLANE = 32
HALO = 3
BLOCK = 128
TINY = 1.1754944e-38
WHOLE = pl.BlockSpec(memory_space=pltpu.VMEM)
SCALARS = pl.BlockSpec(memory_space=pltpu.SMEM)
AWAY = pl.BlockSpec(memory_space=pl.ANY)


class Column:
    def __init__(self):
        self.rows, self.two, self.four = [], [], []

    def feed(self, row):
        rows, two, four = self.rows, self.two, self.four
        rows.append(row)
        at = len(rows) - 1
        if at >= 1:
            two.append(rows[at - 1] + row)
        if at >= 3:
            four.append(two[at - 3] + two[at - 1])
        out = at - HALO
        if out < 0:
            return None
        if out == 0:
            return four[0]
        if out == 1:
            return four[0] + rows[4]
        if out == 2:
            return four[0] + two[4]
        return four[out - 3] + two[out + 1] + row


def band_matrix(ref):
    shape = (BLOCK, 2 * BLOCK)
    source = lax.broadcasted_iota(jnp.int32, shape, 0)
    target = lax.broadcasted_iota(jnp.int32, shape, 1)
    gap = jnp.where(target < BLOCK, jnp.abs(target - source), BLOCK - jnp.abs(target - BLOCK - source))
    ones = (gap <= HALO).astype(jnp.float32).astype(jnp.bfloat16)
    for part in range(3):
        ref[part * BLOCK : (part + 1) * BLOCK, :] = ones


def horizontal(x, band):
    count, blocks, height, _ = x.shape
    x = x.reshape(count * blocks * height, BLOCK)
    high = x.astype(jnp.bfloat16)
    rest = x - high.astype(jnp.float32)
    middle = rest.astype(jnp.bfloat16)
    low = (rest - middle.astype(jnp.float32)).astype(jnp.bfloat16)
    parts = jnp.concatenate([high, middle, low], axis=1)
    got = jnp.dot(parts, band, preferred_element_type=jnp.float32)
    got = got.reshape(count, blocks, height, 2 * BLOCK)
    inside, beside = got[..., :BLOCK], got[..., BLOCK:]
    zero = jnp.zeros_like(beside[:, :1])
    before = jnp.concatenate([zero, beside[:, :-1]], axis=1)
    after = jnp.concatenate([beside[:, 1:], zero], axis=1)
    lane = lax.broadcasted_iota(jnp.int32, beside.shape, 3)
    return inside + jnp.where(lane < BLOCK // 2, before, after)


class Pairs:
    def __init__(self, order, place, own, phase, coher, slots, mine, band, staged, sems):
        self.core = place[0]
        self.phase, self.coher = phase, coher
        self.slots, self.mine, self.band, self.staged, self.sems = slots, mine, band, staged, sems
        self.rows, self.cells = own.shape[0], own.shape[1] // 2
        self.height, self.blocks = self.rows - HALO, own.shape[1] // 2
        for j in range(order.shape[1]):
            slots[order[0, j]] = j
        for row in range(self.rows):
            mine[row] = own[row].astype(jnp.float32)
        band_matrix(band)

    def store(self, sums, index, row, value):
        if value is not None:
            out = row - HALO
            spot = out + self.core * (self.height - 1 - 2 * out)
            sums[index, pl.ds(spot, self.blocks, stride=self.height), :] = value

    def boxes(self, sums, count):
        x = sums[:count].reshape(count, self.blocks, self.height, BLOCK)
        return horizontal(x, self.band[...])

    def own_intensity(self, sums, first):
        column = Column()
        for row in range(self.rows):
            a0, a1 = self.mine[row, : self.cells], self.mine[row, self.cells :]
            self.store(sums, 0, row, column.feed(a0 * a0 + a1 * a1))
        first[...] = self.boxes(sums, 1)[0]

    def copies(self, turn, slot):
        kept, sems = self.staged.at[turn], self.sems.at[turn]
        return (
            pltpu.make_async_copy(kept.at[0:2], self.phase.at[:, slot], sems.at[0]),
            pltpu.make_async_copy(kept.at[2], self.coher.at[slot], sems.at[1]),
        )

    def one(self, other, offset, turn, sums, first):
        slot = self.slots[offset - 1]
        columns = [Column() for _ in range(3)]
        for row in range(self.rows):
            a0, a1 = self.mine[row, : self.cells], self.mine[row, self.cells :]
            b = other(row)
            b0, b1 = b[: self.cells], b[self.cells :]
            values = (a0 * b0 + a1 * b1, a1 * b0 - a0 * b1, b0 * b0 + b1 * b1)
            for index, value in enumerate(values):
                self.store(sums, index, row, columns[index].feed(value))
        re, im, second = self.boxes(sums, 3)
        power = re * re + im * im
        inverse = lax.rsqrt(jnp.maximum(power, TINY))
        scale = jnp.minimum(inverse, 1.0)
        both = first[...] * second
        co = power * inverse * lax.rsqrt(jnp.maximum(both, 1.0))
        for index, value in enumerate((re * scale, im * scale, co)):
            value = value.astype(jnp.bfloat16)
            for b in range(self.blocks):
                self.staged[turn, index, :, b * BLOCK : (b + 1) * BLOCK] = value[b]
        for copy in self.copies(turn, slot):
            copy.start()

    def finish(self, turns):
        for turn in range(turns):
            for copy in self.copies(turn, 0):
                copy.wait()


def first_kernel(order, place, own, eight, _n, _t, phase, coher, first, slots, mine, band, staged, sems, *sums):
    pairs = Pairs(order, place, own, phase, coher, slots, mine, band, staged, sems)
    pairs.own_intensity(sums[1], first)
    pairs.one(lambda row: eight[row].astype(jnp.float32), GROUP, 0, sums[0], first)
    pairs.finish(1)


def near_kernel(order, place, own, near, first, _p, _c, phase, coher, slots, mine, band, staged, sems, *sums):
    pairs = Pairs(order, place, own, phase, coher, slots, mine, band, staged, sems)
    for turn in range(GROUP - 1):
        member = lax.rem(place[1] + 1 + turn, GROUP)
        pairs.one(lambda row: near[member, row].astype(jnp.float32), turn + 1, turn, sums[turn % len(sums)], first)
    pairs.finish(GROUP - 1)


def last_kernel(order, place, own, nine, nine_far, ten, ten_far, first, _p, _c, phase, coher, slots, mine, band, staged, sems, *sums):
    pairs = Pairs(order, place, own, phase, coher, slots, mine, band, staged, sems)
    for turn, (by_group, far) in enumerate(((nine, nine_far), (ten, ten_far)), 0):
        pairs.one(
            lambda row: by_group[row].astype(jnp.float32) + far[row].astype(jnp.float32),
            GROUP + 1 + turn, turn, sums[turn % len(sums)], first,
        )
    pairs.finish(2)


def moved(shard, pairs):
    return lax.ppermute(shard, "date", pairs)


def shards(slc, valid_rows, pair_order):
    _, _, height, width = slc.shape
    band = pair_order.shape[1]
    blocks = width // BLOCK
    cells = 2 * blocks
    rows = height + HALO
    core = lax.axis_index("row")
    rank = lax.rem(lax.axis_index("date"), GROUP)
    length = lax.axis_size("date")
    slab = slc[:, 0] * valid_rows.astype(jnp.bfloat16)[0][None, :, None]
    slab = slab.reshape(2, height, blocks, BLOCK).transpose(1, 0, 2, 3).reshape(height, cells, BLOCK)
    slab = jnp.where(core == 0, slab, slab[::-1])
    halo = lax.ppermute(slab[height - HALO :][::-1], "row", [(0, 1), (1, 0)])
    own = jnp.concatenate([slab, halo], axis=0)
    eight = moved(own, [(i, i - GROUP) for i in range(GROUP, length)])
    ends = range(PLANE, length, PLANE)
    nine_far = moved(own, [(z + GROUP, z - 1) for z in ends])
    ten_far = moved(own, [(z + GROUP + i, z - 2 + i) for z in ends for i in range(2)])
    members = jnp.arange(GROUP)[:, None, None, None]
    given = jnp.where(members < rank, own[None], eight[None])
    groups = [list(range(g, g + GROUP)) for g in range(0, length, GROUP)]
    near = lax.all_to_all(given, "date", 0, 0, axis_index_groups=groups, tiled=True)
    nine, ten = (
        moved(eight, [(i, i - by) for i in range(length) if i % PLANE >= by]) for by in (1, 2)
    )
    place = jnp.stack([core, rank]).astype(jnp.int32)

    outs = (
        jax.ShapeDtypeStruct((2, band, height, width), jnp.bfloat16),
        jax.ShapeDtypeStruct((band, height, width), jnp.bfloat16),
    )
    kept = jax.ShapeDtypeStruct((blocks, height, BLOCK), jnp.float32)

    def scratch(turns, buffers):
        return [
            pltpu.SMEM((band,), jnp.int32),
            pltpu.VMEM((rows, cells, BLOCK), jnp.float32),
            pltpu.VMEM((3 * BLOCK, 2 * BLOCK), jnp.bfloat16),
            pltpu.VMEM((turns, 3, height, width), jnp.bfloat16),
            pltpu.SemaphoreType.DMA((turns, 2)),
        ] + [pltpu.VMEM((3, blocks * height, BLOCK), jnp.float32) for _ in range(buffers)]

    def cost(count):
        return pl.CostEstimate(flops=count << 33, bytes_accessed=count << 23, transcendentals=count << 15)

    params = pltpu.CompilerParams(vmem_limit_bytes=16 << 20)
    phase, coher, first = pl.pallas_call(
        first_kernel,
        out_shape=outs + (kept,),
        in_specs=[SCALARS, SCALARS, WHOLE, WHOLE, AWAY, AWAY],
        out_specs=(AWAY, AWAY, WHOLE),
        scratch_shapes=scratch(1, 2),
        compiler_params=params,
        cost_estimate=cost(3),
    )(pair_order, place, own, eight, nine_far, ten_far)
    phase, coher = pl.pallas_call(
        near_kernel,
        out_shape=outs,
        in_specs=[SCALARS, SCALARS, WHOLE, WHOLE, WHOLE, AWAY, AWAY],
        out_specs=(AWAY, AWAY),
        scratch_shapes=scratch(GROUP - 1, 2),
        input_output_aliases={5: 0, 6: 1},
        compiler_params=params,
        cost_estimate=cost(GROUP - 1),
    )(pair_order, place, own, near, first, phase, coher)
    phase, coher = pl.pallas_call(
        last_kernel,
        out_shape=outs,
        in_specs=[SCALARS, SCALARS] + [WHOLE] * 6 + [AWAY, AWAY],
        out_specs=(AWAY, AWAY),
        scratch_shapes=scratch(2, 2),
        input_output_aliases={8: 0, 9: 1},
        compiler_params=params,
        cost_estimate=cost(2),
    )(pair_order, place, own, nine, nine_far, ten, ten_far, first, phase, coher)
    return phase[:, None], coher[None]


def solution(mesh):
    placed = (P(None, "date", "row", None), P("date", "row"), P("date", None))
    return jax.shard_map(
        shards,
        mesh=mesh,
        in_specs=placed,
        out_specs=(P(None, "date", None, "row", None), P("date", None, "row", None)),
        check_vma=False,
    )
```

```python
import jax
import jax.numpy as jnp
from jax import lax
from jax.experimental import pallas as pl
from jax.experimental.pallas import tpu as pltpu
from jax.sharding import PartitionSpec as P

GROUP = 8
PLANE = 32
LEFT = 3
HALO = 3
BLOCK = 128
TINY = 1.1754944e-38
WHOLE = pl.BlockSpec(memory_space=pltpu.VMEM)
SCALARS = pl.BlockSpec(memory_space=pltpu.SMEM)
AWAY = pl.BlockSpec(memory_space=pl.ANY)


class Column:
    def __init__(self):
        self.rows, self.two, self.four = [], [], []

    def feed(self, row):
        rows, two, four = self.rows, self.two, self.four
        rows.append(row)
        at = len(rows) - 1
        if at >= 1:
            two.append(rows[at - 1] + row)
        if at >= 3:
            four.append(two[at - 3] + two[at - 1])
        out = at - HALO
        if out < 0:
            return None
        if out == 0:
            return four[0]
        if out == 1:
            return four[0] + rows[4]
        if out == 2:
            return four[0] + two[4]
        return four[out - 3] + two[out + 1] + row


def band_matrix(ref):
    shape = (BLOCK, 2 * BLOCK)
    source = lax.broadcasted_iota(jnp.int32, shape, 0)
    target = lax.broadcasted_iota(jnp.int32, shape, 1)
    gap = jnp.where(target < BLOCK, jnp.abs(target - source), BLOCK - jnp.abs(target - BLOCK - source))
    ones = (gap <= HALO).astype(jnp.float32).astype(jnp.bfloat16)
    for part in range(3):
        ref[part * BLOCK : (part + 1) * BLOCK, :] = ones


def horizontal(x, band):
    count, blocks, height, _ = x.shape
    x = x.reshape(count * blocks * height, BLOCK)
    high = x.astype(jnp.bfloat16)
    rest = x - high.astype(jnp.float32)
    middle = rest.astype(jnp.bfloat16)
    low = (rest - middle.astype(jnp.float32)).astype(jnp.bfloat16)
    parts = jnp.concatenate([high, middle, low], axis=1)
    got = jnp.dot(parts, band, preferred_element_type=jnp.float32)
    got = got.reshape(count, blocks, height, 2 * BLOCK)
    inside, beside = got[..., :BLOCK], got[..., BLOCK:]
    zero = jnp.zeros_like(beside[:, :1])
    before = jnp.concatenate([zero, beside[:, :-1]], axis=1)
    after = jnp.concatenate([beside[:, 1:], zero], axis=1)
    lane = lax.broadcasted_iota(jnp.int32, beside.shape, 3)
    return inside + jnp.where(lane < BLOCK // 2, before, after)


class Pairs:
    def __init__(self, order, place, phase, coher, slots, mine, band, staged, sems):
        self.core = place[0]
        self.phase, self.coher = phase, coher
        self.slots, self.mine, self.band, self.staged, self.sems = slots, mine, band, staged, sems
        self.rows, self.cells = mine.shape[0], mine.shape[1] // 2
        self.height, self.blocks = self.rows - HALO, mine.shape[1] // 2
        for j in range(order.shape[1]):
            slots[order[0, j]] = j

    def store(self, sums, index, row, value):
        if value is not None:
            out = row - HALO
            spot = out + self.core * (self.height - 1 - 2 * out)
            sums[index, pl.ds(spot, self.blocks, stride=self.height), :] = value

    def boxes(self, sums, count):
        x = sums[:count].reshape(count, self.blocks, self.height, BLOCK)
        return horizontal(x, self.band[...])

    def own_intensity(self, sums, first):
        column = Column()
        for row in range(self.rows):
            a0, a1 = self.mine[row, : self.cells], self.mine[row, self.cells :]
            self.store(sums, 0, row, column.feed(a0 * a0 + a1 * a1))
        first[...] = self.boxes(sums, 1)[0]

    def copies(self, kept, sem, slot):
        sems = self.sems.at[sem]
        return (
            pltpu.make_async_copy(kept.at[0:2], self.phase.at[:, slot], sems.at[0]),
            pltpu.make_async_copy(kept.at[2], self.coher.at[slot], sems.at[1]),
        )

    def send(self, kept, sem, offset):
        for copy in self.copies(kept, sem, self.slots[offset - 1]):
            copy.start()

    def one(self, other, kept, sums, first):
        columns = [Column() for _ in range(3)]
        for row in range(self.rows):
            a0, a1 = self.mine[row, : self.cells], self.mine[row, self.cells :]
            b = other(row)
            b0, b1 = b[: self.cells], b[self.cells :]
            values = (a0 * b0 + a1 * b1, a1 * b0 - a0 * b1, b0 * b0 + b1 * b1)
            for index, value in enumerate(values):
                self.store(sums, index, row, columns[index].feed(value))
        re, im, second = self.boxes(sums, 3)
        power = re * re + im * im
        inverse = lax.rsqrt(jnp.maximum(power, TINY))
        scale = jnp.minimum(inverse, 1.0)
        both = first[...] * second
        co = power * inverse * lax.rsqrt(jnp.maximum(both, 1.0))
        for index, value in enumerate((re * scale, im * scale, co)):
            value = value.astype(jnp.bfloat16)
            for b in range(self.blocks):
                kept[index, :, b * BLOCK : (b + 1) * BLOCK] = value[b]

    def finish(self, kepts):
        for sem, kept in enumerate(kepts):
            for copy in self.copies(kept, sem, 0):
                copy.wait()


def first_kernel(order, place, own, eight, _n, _t, phase, coher, first, mine, band, slots, staged, sems, *sums):
    for row in range(own.shape[0]):
        mine[row] = own[row].astype(jnp.float32)
    band_matrix(band)
    pairs = Pairs(order, place, phase, coher, slots, mine, band, staged, sems)
    pairs.own_intensity(sums[1], first)
    pairs.one(lambda row: eight[row].astype(jnp.float32), staged.at[0], sums[0], first)
    pairs.send(staged.at[0], 0, GROUP)
    pairs.finish([staged.at[0]])


def near_kernel(order, place, near, first, mine, band, _p, _c, phase, coher, left, slots, staged, sems, *sums):
    pairs = Pairs(order, place, phase, coher, slots, mine, band, staged, sems)
    sent = GROUP - 1 - LEFT
    for turn in range(GROUP - 1):
        member = lax.rem(place[1] + 1 + turn, GROUP)
        kept = staged.at[turn] if turn < sent else left.at[turn - sent]
        pairs.one(lambda row: near[member, row].astype(jnp.float32), kept, sums[turn % len(sums)], first)
        if turn < sent:
            pairs.send(kept, turn, turn + 1)
    pairs.finish([staged.at[turn] for turn in range(sent)])


def last_kernel(order, place, left, nine, nine_far, ten, ten_far, first, mine, band, _p, _c, phase, coher, slots, staged, sems, *sums):
    pairs = Pairs(order, place, phase, coher, slots, mine, band, staged, sems)
    kepts = [left.at[turn] for turn in range(LEFT)] + [staged.at[turn] for turn in range(2)]
    for turn in range(LEFT):
        pairs.send(kepts[turn], turn, GROUP - LEFT + turn)
    for turn, (by_group, far) in enumerate(((nine, nine_far), (ten, ten_far))):
        pairs.one(
            lambda row: by_group[row].astype(jnp.float32) + far[row].astype(jnp.float32),
            kepts[LEFT + turn], sums[turn], first,
        )
        pairs.send(kepts[LEFT + turn], LEFT + turn, GROUP + 1 + turn)
    pairs.finish(kepts)


def moved(shard, pairs):
    return lax.ppermute(shard, "date", pairs)


def shards(slc, valid_rows, pair_order):
    _, _, height, width = slc.shape
    band = pair_order.shape[1]
    blocks = width // BLOCK
    cells = 2 * blocks
    rows = height + HALO
    core = lax.axis_index("row")
    rank = lax.rem(lax.axis_index("date"), GROUP)
    length = lax.axis_size("date")
    slab = slc[:, 0] * valid_rows.astype(jnp.bfloat16)[0][None, :, None]
    slab = slab.reshape(2, height, blocks, BLOCK).transpose(1, 0, 2, 3).reshape(height, cells, BLOCK)
    slab = jnp.where(core == 0, slab, slab[::-1])
    halos = lax.all_gather(slab[height - HALO :][::-1], "row")
    halo = jnp.where(core == 0, halos[1], halos[0])
    own = jnp.concatenate([slab, halo], axis=0)
    eight = moved(own, [(i, i - GROUP) for i in range(GROUP, length)])
    ends = range(PLANE, length, PLANE)
    nine_far = moved(own, [(z + GROUP, z - 1) for z in ends])
    ten_far = moved(own, [(z + GROUP + i, z - 2 + i) for z in ends for i in range(2)])
    members = jnp.arange(GROUP)[:, None, None, None]
    given = jnp.where(members < rank, own[None], eight[None])
    groups = [list(range(g, g + GROUP)) for g in range(0, length, GROUP)]
    near = lax.all_to_all(given, "date", 0, 0, axis_index_groups=groups, tiled=True)
    nine, ten = (
        moved(eight, [(i, i - by) for i in range(length) if i % PLANE >= by]) for by in (1, 2)
    )
    place = jnp.stack([core, rank]).astype(jnp.int32)

    outs = (
        jax.ShapeDtypeStruct((2, band, height, width), jnp.bfloat16),
        jax.ShapeDtypeStruct((band, height, width), jnp.bfloat16),
    )
    kept = jax.ShapeDtypeStruct((blocks, height, BLOCK), jnp.float32)

    def scratch(turns, copies):
        return [
            pltpu.SMEM((band,), jnp.int32),
            pltpu.VMEM((turns, 3, height, width), jnp.bfloat16),
            pltpu.SemaphoreType.DMA((copies, 2)),
        ] + [pltpu.VMEM((3, blocks * height, BLOCK), jnp.float32) for _ in range(2)]

    def cost(count):
        return pl.CostEstimate(flops=count << 33, bytes_accessed=count << 23, transcendentals=count << 15)

    params = pltpu.CompilerParams(vmem_limit_bytes=16 << 20)
    handed = (
        jax.ShapeDtypeStruct((rows, cells, BLOCK), jnp.float32),
        jax.ShapeDtypeStruct((3 * BLOCK, 2 * BLOCK), jnp.bfloat16),
    )
    phase, coher, first, mine, ones = pl.pallas_call(
        first_kernel,
        out_shape=outs + (kept,) + handed,
        in_specs=[SCALARS, SCALARS, WHOLE, WHOLE, AWAY, AWAY],
        out_specs=(AWAY, AWAY, WHOLE, WHOLE, WHOLE),
        scratch_shapes=scratch(1, 1),
        compiler_params=params,
        cost_estimate=cost(3),
    )(pair_order, place, own, eight, nine_far, ten_far)
    phase, coher, left = pl.pallas_call(
        near_kernel,
        out_shape=outs + (jax.ShapeDtypeStruct((LEFT, 3, height, width), jnp.bfloat16),),
        in_specs=[SCALARS, SCALARS] + [WHOLE] * 4 + [AWAY, AWAY],
        out_specs=(AWAY, AWAY, WHOLE),
        scratch_shapes=scratch(GROUP - 1 - LEFT, GROUP - 1 - LEFT),
        input_output_aliases={6: 0, 7: 1},
        compiler_params=params,
        cost_estimate=cost(GROUP - 1),
    )(pair_order, place, near, first, mine, ones, phase, coher)
    phase, coher = pl.pallas_call(
        last_kernel,
        out_shape=outs,
        in_specs=[SCALARS, SCALARS] + [WHOLE] * 8 + [AWAY, AWAY],
        out_specs=(AWAY, AWAY),
        scratch_shapes=scratch(2, LEFT + 2),
        input_output_aliases={10: 0, 11: 1},
        compiler_params=params,
        cost_estimate=cost(2),
    )(pair_order, place, left, nine, nine_far, ten, ten_far, first, mine, ones, phase, coher)
    return phase[:, None], coher[None]


def solution(mesh):
    placed = (P(None, "date", "row", None), P("date", "row"), P("date", None))
    return jax.shard_map(
        shards,
        mesh=mesh,
        in_specs=placed,
        out_specs=(P(None, "date", None, "row", None), P("date", None, "row", None)),
        check_vma=False,
    )
```

```python
import jax
import jax.numpy as jnp
from jax import lax
from jax.experimental import pallas as pl
from jax.experimental.pallas import tpu as pltpu
from jax.sharding import PartitionSpec as P

GROUP = 8
PLANE = 32
LEFT = 5
HALO = 3
BLOCK = 128
TINY = 1.1754944e-38
WHOLE = pl.BlockSpec(memory_space=pltpu.VMEM)
SCALARS = pl.BlockSpec(memory_space=pltpu.SMEM)
AWAY = pl.BlockSpec(memory_space=pl.ANY)


class Column:
    def __init__(self):
        self.rows, self.two, self.four = [], [], []

    def feed(self, row):
        rows, two, four = self.rows, self.two, self.four
        rows.append(row)
        at = len(rows) - 1
        if at >= 1:
            two.append(rows[at - 1] + row)
        if at >= 3:
            four.append(two[at - 3] + two[at - 1])
        out = at - HALO
        if out < 0:
            return None
        if out == 0:
            return four[0]
        if out == 1:
            return four[0] + rows[4]
        if out == 2:
            return four[0] + two[4]
        return four[out - 3] + two[out + 1] + row


def band_matrix(ref):
    shape = (BLOCK, 2 * BLOCK)
    source = lax.broadcasted_iota(jnp.int32, shape, 0)
    target = lax.broadcasted_iota(jnp.int32, shape, 1)
    gap = jnp.where(target < BLOCK, jnp.abs(target - source), BLOCK - jnp.abs(target - BLOCK - source))
    ones = (gap <= HALO).astype(jnp.float32).astype(jnp.bfloat16)
    for part in range(3):
        ref[part * BLOCK : (part + 1) * BLOCK, :] = ones


def horizontal(x, band):
    count, blocks, height, _ = x.shape
    x = x.reshape(count * blocks * height, BLOCK)
    high = x.astype(jnp.bfloat16)
    rest = x - high.astype(jnp.float32)
    middle = rest.astype(jnp.bfloat16)
    low = (rest - middle.astype(jnp.float32)).astype(jnp.bfloat16)
    parts = jnp.concatenate([high, middle, low], axis=1)
    got = jnp.dot(parts, band, preferred_element_type=jnp.float32)
    got = got.reshape(count, blocks, height, 2 * BLOCK)
    inside, beside = got[..., :BLOCK], got[..., BLOCK:]
    zero = jnp.zeros_like(beside[:, :1])
    before = jnp.concatenate([zero, beside[:, :-1]], axis=1)
    after = jnp.concatenate([beside[:, 1:], zero], axis=1)
    lane = lax.broadcasted_iota(jnp.int32, beside.shape, 3)
    return inside + jnp.where(lane < BLOCK // 2, before, after)


class Pairs:
    def __init__(self, order, place, phase, coher, slots, mine, band, staged, sems):
        self.core = place[0]
        self.phase, self.coher = phase, coher
        self.slots, self.mine, self.band, self.staged, self.sems = slots, mine, band, staged, sems
        self.rows, self.cells = mine.shape[0], mine.shape[1] // 2
        self.height, self.blocks = self.rows - HALO, mine.shape[1] // 2
        for j in range(order.shape[1]):
            slots[order[0, j]] = j

    def store(self, sums, index, row, value):
        if value is not None:
            out = row - HALO
            spot = out + self.core * (self.height - 1 - 2 * out)
            sums[index, pl.ds(spot, self.blocks, stride=self.height), :] = value

    def boxes(self, sums, count):
        x = sums[:count].reshape(count, self.blocks, self.height, BLOCK)
        return horizontal(x, self.band[...])

    def own_intensity(self, sums, first):
        column = Column()
        for row in range(self.rows):
            a0, a1 = self.mine[row, : self.cells], self.mine[row, self.cells :]
            self.store(sums, 0, row, column.feed(a0 * a0 + a1 * a1))
        first[...] = self.boxes(sums, 1)[0]

    def copies(self, kept, sem, slot):
        sems = self.sems.at[sem]
        return (
            pltpu.make_async_copy(kept.at[0:2], self.phase.at[:, slot], sems.at[0]),
            pltpu.make_async_copy(kept.at[2], self.coher.at[slot], sems.at[1]),
        )

    def send(self, kept, sem, offset):
        for copy in self.copies(kept, sem, self.slots[offset - 1]):
            copy.start()

    def one(self, other, kept, sums, first):
        columns = [Column() for _ in range(3)]
        for row in range(self.rows):
            a0, a1 = self.mine[row, : self.cells], self.mine[row, self.cells :]
            b = other(row)
            b0, b1 = b[: self.cells], b[self.cells :]
            values = (a0 * b0 + a1 * b1, a1 * b0 - a0 * b1, b0 * b0 + b1 * b1)
            for index, value in enumerate(values):
                self.store(sums, index, row, columns[index].feed(value))
        re, im, second = self.boxes(sums, 3)
        power = re * re + im * im
        inverse = lax.rsqrt(jnp.maximum(power, TINY))
        scale = jnp.minimum(inverse, 1.0)
        both = first[...] * second
        co = power * inverse * lax.rsqrt(jnp.maximum(both, 1.0))
        for index, value in enumerate((re * scale, im * scale, co)):
            value = value.astype(jnp.bfloat16)
            for b in range(self.blocks):
                kept[index, :, b * BLOCK : (b + 1) * BLOCK] = value[b]

    def finish(self, kepts):
        for sem, kept in enumerate(kepts):
            for copy in self.copies(kept, sem, 0):
                copy.wait()


def first_kernel(order, place, own, eight, _n, _t, phase, coher, first, mine, band, slots, staged, sems, *sums):
    for row in range(own.shape[0]):
        mine[row] = own[row].astype(jnp.float32)
    band_matrix(band)
    pairs = Pairs(order, place, phase, coher, slots, mine, band, staged, sems)
    pairs.own_intensity(sums[1], first)
    pairs.one(lambda row: eight[row].astype(jnp.float32), staged.at[0], sums[0], first)
    pairs.send(staged.at[0], 0, GROUP)
    pairs.finish([staged.at[0]])


def near_kernel(order, place, near, first, mine, band, _p, _c, phase, coher, left, slots, staged, sems, *sums):
    pairs = Pairs(order, place, phase, coher, slots, mine, band, staged, sems)
    sent = GROUP - 1 - LEFT
    for turn in range(GROUP - 1):
        member = lax.rem(place[1] + 1 + turn, GROUP)
        kept = staged.at[turn] if turn < sent else left.at[turn - sent]
        pairs.one(lambda row: near[member, row].astype(jnp.float32), kept, sums[turn % len(sums)], first)
        if turn < sent:
            pairs.send(kept, turn, turn + 1)
    pairs.finish([staged.at[turn] for turn in range(sent)])


def last_kernel(order, place, left, nine, nine_far, ten, ten_far, first, mine, band, _p, _c, phase, coher, slots, staged, sems, *sums):
    pairs = Pairs(order, place, phase, coher, slots, mine, band, staged, sems)
    kepts = [left.at[turn] for turn in range(LEFT)] + [staged.at[turn] for turn in range(2)]
    for turn in range(LEFT):
        pairs.send(kepts[turn], turn, GROUP - LEFT + turn)
    for turn, (by_group, far) in enumerate(((nine, nine_far), (ten, ten_far))):
        pairs.one(
            lambda row: by_group[row].astype(jnp.float32) + far[row].astype(jnp.float32),
            kepts[LEFT + turn], sums[turn], first,
        )
    for turn in range(2):
        pairs.send(kepts[LEFT + turn], LEFT + turn, GROUP + 1 + turn)
    pairs.finish(kepts)


def moved(shard, pairs):
    return lax.ppermute(shard, "date", pairs)


def shards(slc, valid_rows, pair_order):
    _, _, height, width = slc.shape
    band = pair_order.shape[1]
    blocks = width // BLOCK
    cells = 2 * blocks
    rows = height + HALO
    core = lax.axis_index("row")
    rank = lax.rem(lax.axis_index("date"), GROUP)
    length = lax.axis_size("date")
    slab = slc[:, 0] * valid_rows.astype(jnp.bfloat16)[0][None, :, None]
    slab = slab.reshape(2, height, blocks, BLOCK).transpose(1, 0, 2, 3).reshape(height, cells, BLOCK)
    slab = jnp.where(core == 0, slab, slab[::-1])
    halos = lax.all_gather(slab[height - HALO :][::-1], "row")
    halo = jnp.where(core == 0, halos[1], halos[0])
    own = jnp.concatenate([slab, halo], axis=0)
    eight = moved(own, [(i, i - GROUP) for i in range(GROUP, length)])
    ends = range(PLANE, length, PLANE)
    nine_far = moved(own, [(z + GROUP, z - 1) for z in ends])
    ten_far = moved(own, [(z + GROUP + i, z - 2 + i) for z in ends for i in range(2)])
    members = jnp.arange(GROUP)[:, None, None, None]
    given = jnp.where(members < rank, own[None], eight[None])
    groups = [list(range(g, g + GROUP)) for g in range(0, length, GROUP)]
    near = lax.all_to_all(given, "date", 0, 0, axis_index_groups=groups, tiled=True)
    nine, ten = (
        moved(eight, [(i, i - by) for i in range(length) if i % PLANE >= by]) for by in (1, 2)
    )
    place = jnp.stack([core, rank]).astype(jnp.int32)

    outs = (
        jax.ShapeDtypeStruct((2, band, height, width), jnp.bfloat16),
        jax.ShapeDtypeStruct((band, height, width), jnp.bfloat16),
    )
    kept = jax.ShapeDtypeStruct((blocks, height, BLOCK), jnp.float32)

    def scratch(turns, copies):
        return [
            pltpu.SMEM((band,), jnp.int32),
            pltpu.VMEM((turns, 3, height, width), jnp.bfloat16),
            pltpu.SemaphoreType.DMA((copies, 2)),
        ] + [pltpu.VMEM((3, blocks * height, BLOCK), jnp.float32) for _ in range(2)]

    def cost(count):
        return pl.CostEstimate(flops=count << 33, bytes_accessed=count << 23, transcendentals=count << 15)

    params = pltpu.CompilerParams(vmem_limit_bytes=16 << 20)
    handed = (
        jax.ShapeDtypeStruct((rows, cells, BLOCK), jnp.float32),
        jax.ShapeDtypeStruct((3 * BLOCK, 2 * BLOCK), jnp.bfloat16),
    )
    phase, coher, first, mine, ones = pl.pallas_call(
        first_kernel,
        out_shape=outs + (kept,) + handed,
        in_specs=[SCALARS, SCALARS, WHOLE, WHOLE, AWAY, AWAY],
        out_specs=(AWAY, AWAY, WHOLE, WHOLE, WHOLE),
        scratch_shapes=scratch(1, 1),
        compiler_params=params,
        cost_estimate=cost(3),
    )(pair_order, place, own, eight, nine_far, ten_far)
    phase, coher, left = pl.pallas_call(
        near_kernel,
        out_shape=outs + (jax.ShapeDtypeStruct((LEFT, 3, height, width), jnp.bfloat16),),
        in_specs=[SCALARS, SCALARS] + [WHOLE] * 4 + [AWAY, AWAY],
        out_specs=(AWAY, AWAY, WHOLE),
        scratch_shapes=scratch(GROUP - 1 - LEFT, GROUP - 1 - LEFT),
        input_output_aliases={6: 0, 7: 1},
        compiler_params=params,
        cost_estimate=cost(GROUP - 1),
    )(pair_order, place, near, first, mine, ones, phase, coher)
    phase, coher = pl.pallas_call(
        last_kernel,
        out_shape=outs,
        in_specs=[SCALARS, SCALARS] + [WHOLE] * 8 + [AWAY, AWAY],
        out_specs=(AWAY, AWAY),
        scratch_shapes=scratch(2, LEFT + 2),
        input_output_aliases={10: 0, 11: 1},
        compiler_params=params,
        cost_estimate=cost(2),
    )(pair_order, place, left, nine, nine_far, ten, ten_far, first, mine, ones, phase, coher)
    return phase[:, None], coher[None]


def solution(mesh):
    placed = (P(None, "date", "row", None), P("date", "row"), P("date", None))
    return jax.shard_map(
        shards,
        mesh=mesh,
        in_specs=placed,
        out_specs=(P(None, "date", None, "row", None), P("date", None, "row", None)),
        check_vma=False,
    )
```

```python
import jax
import jax.numpy as jnp
from jax import lax
from jax.experimental import pallas as pl
from jax.experimental.pallas import tpu as pltpu
from jax.sharding import PartitionSpec as P

GROUP = 8
PLANE = 32
LEFT = 3
HALO = 3
BLOCK = 128
TINY = 1.1754944e-38
WHOLE = pl.BlockSpec(memory_space=pltpu.VMEM)
SCALARS = pl.BlockSpec(memory_space=pltpu.SMEM)
AWAY = pl.BlockSpec(memory_space=pl.ANY)


class Column:
    def __init__(self):
        self.rows, self.two, self.four = [], [], []

    def feed(self, row):
        rows, two, four = self.rows, self.two, self.four
        rows.append(row)
        at = len(rows) - 1
        if at >= 1:
            two.append(rows[at - 1] + row)
        if at >= 3:
            four.append(two[at - 3] + two[at - 1])
        out = at - HALO
        if out < 0:
            return None
        if out == 0:
            return four[0]
        if out == 1:
            return four[0] + rows[4]
        if out == 2:
            return four[0] + two[4]
        return four[out - 3] + two[out + 1] + row


def band_matrix(ref):
    shape = (BLOCK, 2 * BLOCK)
    source = lax.broadcasted_iota(jnp.int32, shape, 0)
    target = lax.broadcasted_iota(jnp.int32, shape, 1)
    gap = jnp.where(target < BLOCK, jnp.abs(target - source), BLOCK - jnp.abs(target - BLOCK - source))
    ones = (gap <= HALO).astype(jnp.float32).astype(jnp.bfloat16)
    for part in range(3):
        ref[part * BLOCK : (part + 1) * BLOCK, :] = ones


def horizontal(x, band):
    count, blocks, height, _ = x.shape
    x = x.reshape(count * blocks * height, BLOCK)
    high = x.astype(jnp.bfloat16)
    rest = x - high.astype(jnp.float32)
    middle = rest.astype(jnp.bfloat16)
    low = (rest - middle.astype(jnp.float32)).astype(jnp.bfloat16)
    parts = jnp.concatenate([high, middle, low], axis=1)
    got = jnp.dot(parts, band, preferred_element_type=jnp.float32)
    got = got.reshape(count, blocks, height, 2 * BLOCK)
    inside, beside = got[..., :BLOCK], got[..., BLOCK:]
    zero = jnp.zeros_like(beside[:, :1])
    before = jnp.concatenate([zero, beside[:, :-1]], axis=1)
    after = jnp.concatenate([beside[:, 1:], zero], axis=1)
    lane = lax.broadcasted_iota(jnp.int32, beside.shape, 3)
    return inside + jnp.where(lane < BLOCK // 2, before, after)


class Pairs:
    def __init__(self, order, place, phase, coher, slots, mine, band, staged, sems):
        self.core = place[0]
        self.phase, self.coher = phase, coher
        self.slots, self.mine, self.band, self.staged, self.sems = slots, mine, band, staged, sems
        self.rows, self.cells = mine.shape[0], mine.shape[1] // 2
        self.height, self.blocks = self.rows - HALO, mine.shape[1] // 2
        for j in range(order.shape[1]):
            slots[order[0, j]] = j

    def store(self, sums, index, row, value):
        if value is not None:
            out = row - HALO
            spot = out + self.core * (self.height - 1 - 2 * out)
            sums[index, pl.ds(spot, self.blocks, stride=self.height), :] = value

    def boxes(self, sums, count):
        x = sums[:count].reshape(count, self.blocks, self.height, BLOCK)
        return horizontal(x, self.band[...])

    def own_intensity(self, sums, first):
        column = Column()
        for row in range(self.rows):
            a0, a1 = self.mine[row, : self.cells], self.mine[row, self.cells :]
            self.store(sums, 0, row, column.feed(a0 * a0 + a1 * a1))
        first[...] = self.boxes(sums, 1)[0]

    def copies(self, kept, sem, slot):
        sems = self.sems.at[sem]
        return (
            pltpu.make_async_copy(kept.at[0:2], self.phase.at[:, slot], sems.at[0]),
            pltpu.make_async_copy(kept.at[2], self.coher.at[slot], sems.at[1]),
        )

    def send(self, kept, sem, offset):
        for copy in self.copies(kept, sem, self.slots[offset - 1]):
            copy.start()

    def one(self, other, kept, sums, first):
        columns = [Column() for _ in range(3)]
        for row in range(self.rows):
            a0, a1 = self.mine[row, : self.cells], self.mine[row, self.cells :]
            b = other(row)
            b0, b1 = b[: self.cells], b[self.cells :]
            values = (a0 * b0 + a1 * b1, a1 * b0 - a0 * b1, b0 * b0 + b1 * b1)
            for index, value in enumerate(values):
                self.store(sums, index, row, columns[index].feed(value))
        re, im, second = self.boxes(sums, 3)
        power = re * re + im * im
        inverse = lax.rsqrt(jnp.maximum(power, TINY))
        scale = jnp.minimum(inverse, 1.0)
        both = first[...] * second
        co = power * inverse * lax.rsqrt(jnp.maximum(both, 1.0))
        for index, value in enumerate((re * scale, im * scale, co)):
            value = value.astype(jnp.bfloat16)
            for b in range(self.blocks):
                kept[index, :, b * BLOCK : (b + 1) * BLOCK] = value[b]

    def finish(self, kepts):
        for sem, kept in enumerate(kepts):
            for copy in self.copies(kept, sem, 0):
                copy.wait()


def first_kernel(order, place, own, eight, _n, _t, phase, coher, first, mine, band, slots, staged, sems, *sums):
    for row in range(own.shape[0]):
        mine[row] = own[row].astype(jnp.float32)
    band_matrix(band)
    pairs = Pairs(order, place, phase, coher, slots, mine, band, staged, sems)
    pairs.own_intensity(sums[1], first)
    pairs.one(lambda row: eight[row].astype(jnp.float32), staged.at[0], sums[0], first)
    pairs.send(staged.at[0], 0, GROUP)
    pairs.finish([staged.at[0]])


def near_kernel(order, place, near, first, mine, band, _p, _c, phase, coher, left, slots, staged, sems, *sums):
    pairs = Pairs(order, place, phase, coher, slots, mine, band, staged, sems)
    sent = GROUP - 1 - LEFT
    for turn in range(GROUP - 1):
        member = lax.rem(place[1] + 1 + turn, GROUP)
        kept = staged.at[turn] if turn < sent else left.at[turn - sent]
        pairs.one(lambda row: near[member, row].astype(jnp.float32), kept, sums[turn % len(sums)], first)
        if turn < sent:
            pairs.send(kept, turn, turn + 1)
    pairs.finish([staged.at[turn] for turn in range(sent)])


def last_kernel(order, place, left, nine, nine_far, ten, ten_far, first, mine, band, _p, _c, phase, coher, slots, staged, sems, *sums):
    pairs = Pairs(order, place, phase, coher, slots, mine, band, staged, sems)
    kepts = [left.at[turn] for turn in range(LEFT)] + [staged.at[turn] for turn in range(2)]
    for turn in range(LEFT):
        pairs.send(kepts[turn], turn, GROUP - LEFT + turn)
    for turn, (by_group, far) in enumerate(((nine, nine_far), (ten, ten_far))):
        pairs.one(
            lambda row: by_group[row].astype(jnp.float32) + far[row].astype(jnp.float32),
            kepts[LEFT + turn], sums[turn], first,
        )
    for turn in range(2):
        pairs.send(kepts[LEFT + turn], LEFT + turn, GROUP + 1 + turn)
    pairs.finish(kepts)


def moved(shard, pairs):
    return lax.ppermute(shard, "date", pairs)


def shards(slc, valid_rows, pair_order):
    _, _, height, width = slc.shape
    band = pair_order.shape[1]
    blocks = width // BLOCK
    cells = 2 * blocks
    rows = height + HALO
    core = lax.axis_index("row")
    rank = lax.rem(lax.axis_index("date"), GROUP)
    length = lax.axis_size("date")
    slab = slc[:, 0] * valid_rows.astype(jnp.bfloat16)[0][None, :, None]
    slab = slab.reshape(2, height, blocks, BLOCK).transpose(1, 0, 2, 3).reshape(height, cells, BLOCK)
    slab = jnp.where(core == 0, slab, slab[::-1])
    halos = lax.all_gather(slab[height - HALO :][::-1], "row")
    halo = jnp.where(core == 0, halos[1], halos[0])
    own = jnp.concatenate([slab, halo], axis=0)
    eight = moved(own, [(i, i - GROUP) for i in range(GROUP, length)])
    ends = range(PLANE, length, PLANE)
    nine_far = moved(own, [(z + GROUP, z - 1) for z in ends])
    ten_far = moved(own, [(z + GROUP + i, z - 2 + i) for z in ends for i in range(2)])
    members = jnp.arange(GROUP)[:, None, None, None]
    given = jnp.where(members < rank, own[None], eight[None])
    groups = [list(range(g, g + GROUP)) for g in range(0, length, GROUP)]
    near = lax.all_to_all(given, "date", 0, 0, axis_index_groups=groups, tiled=True)
    nine, ten = (
        moved(eight, [(i, i - by) for i in range(length) if i % PLANE >= by]) for by in (1, 2)
    )
    place = jnp.stack([core, rank]).astype(jnp.int32)

    outs = (
        jax.ShapeDtypeStruct((2, band, height, width), jnp.bfloat16),
        jax.ShapeDtypeStruct((band, height, width), jnp.bfloat16),
    )
    kept = jax.ShapeDtypeStruct((blocks, height, BLOCK), jnp.float32)

    def scratch(turns, copies):
        return [
            pltpu.SMEM((band,), jnp.int32),
            pltpu.VMEM((turns, 3, height, width), jnp.bfloat16),
            pltpu.SemaphoreType.DMA((copies, 2)),
        ] + [pltpu.VMEM((3, blocks * height, BLOCK), jnp.float32) for _ in range(2)]

    def cost(count):
        return pl.CostEstimate(flops=count << 33, bytes_accessed=count << 23, transcendentals=count << 15)

    params = pltpu.CompilerParams(vmem_limit_bytes=16 << 20)
    handed = (
        jax.ShapeDtypeStruct((rows, cells, BLOCK), jnp.float32),
        jax.ShapeDtypeStruct((3 * BLOCK, 2 * BLOCK), jnp.bfloat16),
    )
    phase, coher, first, mine, ones = pl.pallas_call(
        first_kernel,
        out_shape=outs + (kept,) + handed,
        in_specs=[SCALARS, SCALARS, WHOLE, WHOLE, AWAY, AWAY],
        out_specs=(AWAY, AWAY, WHOLE, WHOLE, WHOLE),
        scratch_shapes=scratch(1, 1),
        compiler_params=params,
        cost_estimate=cost(3),
    )(pair_order, place, own, eight, nine_far, ten_far)
    phase, coher, left = pl.pallas_call(
        near_kernel,
        out_shape=outs + (jax.ShapeDtypeStruct((LEFT, 3, height, width), jnp.bfloat16),),
        in_specs=[SCALARS, SCALARS] + [WHOLE] * 4 + [AWAY, AWAY],
        out_specs=(AWAY, AWAY, WHOLE),
        scratch_shapes=scratch(GROUP - 1 - LEFT, GROUP - 1 - LEFT),
        input_output_aliases={6: 0, 7: 1},
        compiler_params=params,
        cost_estimate=cost(GROUP - 1),
    )(pair_order, place, near, first, mine, ones, phase, coher)
    phase, coher = pl.pallas_call(
        last_kernel,
        out_shape=outs,
        in_specs=[SCALARS, SCALARS] + [WHOLE] * 8 + [AWAY, AWAY],
        out_specs=(AWAY, AWAY),
        scratch_shapes=scratch(2, LEFT + 2),
        input_output_aliases={10: 0, 11: 1},
        compiler_params=params,
        cost_estimate=cost(2),
    )(pair_order, place, left, nine, nine_far, ten, ten_far, first, mine, ones, phase, coher)
    return phase[:, None], coher[None]


def solution(mesh):
    placed = (P(None, "date", "row", None), P("date", "row"), P("date", None))
    return jax.shard_map(
        shards,
        mesh=mesh,
        in_specs=placed,
        out_specs=(P(None, "date", None, "row", None), P("date", None, "row", None)),
        check_vma=False,
    )
```
